256 devices in a mesh: section: 32 (over z_hi, y, core), dp: 8 (over z_lo, x).
Axes of the slice: x: 4, y: 4, z: 8 (z_hi: 4, z_lo: 2; z = z_hi * 2 + z_lo), core: 2. Of those that a mesh axis runs over, the one named last changes fastest.
Arguments:
- activations: bfloat16 [32, 64, 64, 4096], P('section', 'dp'), may hold values from -6 to 6
- out_grads: bfloat16 [32, 64, 64, 4096], P('section', 'dp'), may hold values from -6 to 6
- proj_in: bfloat16 [32, 2, 4096, 128], P('section'), may hold values from -0.09375 to 0.09375
- proj_out: bfloat16 [32, 2, 64, 4096], P('section'), may hold values from -0.09375 to 0.09375
- earlier_gram: float32 [8192, 8192], P('section', 'dp'), may hold values from -4 to 4, as said below
Outputs:
- gram: float32 [8192, 8192], P('section', 'dp')
The draws below stay inside these ranges and needn't reach their ends.
Inputs may be any that keep to these rules, and one draw needn't show every extreme that they name: earlier_gram is symmetric.
All inputs are finite; a program needn't handle non-finite values.
Results may differ from the reference program's by a relative error of at most 0.0013.
Values sent between devices are 32-bit elements; how exact they have to be, the bound alone decides.
No kernel may reach another device: no remote copies, remote signals or barrier semaphores. Data moves between devices by JAX's collectives and lax.ppermute only.
A program may use at most 64 MiB of HBM per device.

```python
import math
import jax
import jax.numpy as jnp
from jax import lax

D = 4096
K_IN = 128
K_OUT = 64
PROJ = 2
LEN = 64
LAYERS = 32
EXAMPLES = 64
K = 8192


def draw_earlier_gram(key, part):
    noise = jax.random.normal(jax.random.fold_in(key, 17), (K, K), jnp.float32)
    return jnp.clip((noise + noise.T) * 0.5, -4.0, 4.0)


def steps_of(stream_key, shape, cuts, least, largest):
    gain = 1.0
    for position, parts in cuts:
        heights = jax.random.uniform(jax.random.fold_in(jax.random.fold_in(stream_key, 6), position), (parts,), jnp.float32, least / len(cuts), largest / len(cuts))
        gain = gain * jnp.repeat(jnp.exp(heights), shape[position] // parts).reshape((-1,) + (1,) * (len(shape) - 1 - position))
    return gain


def centred(rng, shape, deviation, most, shards=(), kind=jnp.bfloat16):
    drawn = deviation * jax.random.normal(rng, shape, jnp.float32)
    if shards:
        drawn = drawn * steps_of(rng, shape, shards, -0.22, 0.18)
    return jnp.clip(drawn, -most, most).astype(kind)


def setup_inputs(seed: int = 0) -> dict:
    key_list = jax.random.split(jax.random.key(seed), 6)
    return {
        "activations": centred(key_list[0], (LAYERS, EXAMPLES, LEN, D), 1.0, 6.0, ((0, 32), (1, 8))),
        "out_grads": centred(key_list[1], (LAYERS, EXAMPLES, LEN, D), 1.0, 6.0, ((0, 32), (1, 8))),
        "proj_in": centred(key_list[2], (LAYERS, PROJ, D, K_IN), D ** -0.5, 0.09375, ((0, 32),)),
        "proj_out": centred(key_list[3], (LAYERS, PROJ, K_OUT, D), D ** -0.5, 0.09375, ((0, 32),)),
        "earlier_gram": draw_earlier_gram(jax.random.fold_in(key_list[5], 71), 0),
    }


def reference(activations, out_grads, proj_in, proj_out, earlier_gram):

    def layer_step(total, inputs):
        layer_act, layer_grad, layer_in, layer_out = inputs
        low_in = jnp.einsum('eld,pdm->pelm', layer_act.astype(jnp.float32), layer_in.astype(jnp.float32)).astype(jnp.bfloat16)
        low_out = jnp.einsum('pkd,eld->pekl', layer_out.astype(jnp.float32), layer_grad.astype(jnp.float32)).astype(jnp.bfloat16)
        partial_terms = jnp.einsum('pekl,pelm->ekm', low_out.astype(jnp.float32), low_in.astype(jnp.float32))
        return (total + partial_terms.reshape(partial_terms.shape[0], -1), None)
    start = jnp.zeros((EXAMPLES, K_OUT * K_IN), jnp.float32)
    summed, unused = lax.scan(layer_step, start, (activations, out_grads, proj_in, proj_out))
    features = summed / math.sqrt(LEN * LAYERS * PROJ)
    outer = jnp.dot(features.T, features, precision=lax.Precision.HIGHEST)
    return earlier_gram + outer / EXAMPLES
```

```python
import jax
import jax.numpy as jnp
from jax import lax
from jax.sharding import PartitionSpec as P

PROJ = 2
LEN = 64
BOTH = ("section", "dp")
ZH, Y, C, ZL, X = 4, 4, 2, 2, 4
SECTIONS, GROUPS = ZH * Y * C, ZL * X
PAIRS = SECTIONS // C


def device_at(zh, y, c, zl, x):
    return ((zh * Y + y) * C + c) * GROUPS + zl * X + x


def first_half(y, d):
    t = (y - 2 * (d % 2)) % 4
    return (t == 1) | (t == 2)


def column_routes(turn):
    pairs = []
    for zh in range(ZH):
        for y in range(Y):
            for zl in range(ZL):
                for x in range(X):
                    d = zl * X + x
                    from_zh = d // 2
                    t = (y - 2 * (d % 2)) % 4
                    half = int(first_half(y, d)) ^ turn
                    from_y = 2 * (d % 2) + half
                    from_x = (x + 2 - (zh - from_zh)) % X
                    from_zl = zl if t >= 2 else 1 - zl
                    for c in range(C):
                        pairs.append(
                            (
                                device_at(from_zh, from_y, c, from_zl, from_x),
                                device_at(zh, y, c, zl, x),
                            )
                        )
    return pairs


ACROSS_CORES = [(s, s ^ 1) for s in range(SECTIONS)]
SAME_CORE = [[p * C + c for p in range(PAIRS)] for c in range(C)]


def per_device(activations, out_grads, proj_in, proj_out, earlier_gram):
    section = lax.axis_index("section")
    dp = lax.axis_index("dp")
    core = section % C
    y = (section // C) % Y
    low_in = jnp.einsum(
        "etd,pdm->petm", activations[0], proj_in[0], preferred_element_type=jnp.float32
    ).astype(jnp.bfloat16)
    low_out = jnp.einsum(
        "pkd,etd->pekt", proj_out[0], out_grads[0], preferred_element_type=jnp.float32
    ).astype(jnp.bfloat16)
    terms = jnp.einsum(
        "pekt,petm->ekm", low_out, low_in, preferred_element_type=jnp.float32
    )
    count = terms.shape[0]
    half = count // C
    terms = terms.reshape(count, -1)
    width = terms.shape[1]
    pair_width = width // PAIRS
    row_width = earlier_gram.shape[0]

    theirs = lax.dynamic_slice_in_dim(terms, (1 - core) * half, half, 0)
    mine = lax.dynamic_slice_in_dim(terms, core * half, half, 0)
    mine = mine + lax.ppermute(theirs, "section", ACROSS_CORES)
    pieces = mine.reshape(half, PAIRS, pair_width).transpose(1, 0, 2)
    pieces = lax.all_to_all(pieces, "section", 0, 0, axis_index_groups=SAME_CORE)
    reduced = pieces.sum(0)
    rows = lax.all_to_all(
        jnp.broadcast_to(reduced, (GROUPS, half, pair_width)), "dp", 0, 0
    )
    rows = rows.reshape(GROUPS * half, pair_width)
    row_mine = lax.dynamic_slice_in_dim(rows, core * row_width, row_width, 1)
    row_theirs = lax.dynamic_slice_in_dim(rows, (1 - core) * row_width, row_width, 1)
    row_other = lax.ppermute(row_theirs, "section", ACROSS_CORES)
    got = [lax.ppermute(rows, BOTH, column_routes(turn)) for turn in range(2)]
    swap = first_half(y, dp)
    cols = jnp.concatenate(
        [jnp.where(swap, got[1], got[0]), jnp.where(swap, got[0], got[1])], 1
    )
    cols_other = lax.ppermute(cols, "section", ACROSS_CORES)
    row_block = jnp.concatenate([row_mine, row_other], 0)
    col_block = jnp.concatenate([cols, cols_other], 0)
    outer = jnp.dot(row_block.T, col_block, precision=lax.Precision.HIGHEST)
    total_examples = count * GROUPS
    return earlier_gram + outer * (1.0 / (LEN * SECTIONS * PROJ * total_examples))


def solution(mesh):
    return jax.shard_map(
        per_device,
        mesh=mesh,
        in_specs=(
            P("section", "dp", None, None),
            P("section", "dp", None, None),
            P("section", None, None, None),
            P("section", None, None, None),
            P("section", "dp"),
        ),
        out_specs=P("section", "dp"),
        check_vma=False,
    )
```

```python
import functools

import jax
import jax.numpy as jnp
from jax import lax
from jax.experimental import pallas as pl
from jax.experimental.pallas import tpu as pltpu
from jax.sharding import PartitionSpec as P

PROJ = 2
LEN = 64
LANES = 128
BOTH = ("section", "dp")
ZH, Y, C, ZL, X = 4, 4, 2, 2, 4
SECTIONS, GROUPS = ZH * Y * C, ZL * X
PAIRS = SECTIONS // C
CHUNK = 512
VMEM_BYTES = 53 * 2**20
F32 = jnp.float32


def device_at(zh, y, c, zl, x):
    return ((zh * Y + y) * C + c) * GROUPS + zl * X + x


ROUTES = [(10, 0), (34, 1), (67, 2), (99, 3), (137, 4), (161, 5), (204, 6), (239, 7), (25, 8), (58, 9), (83, 10), (122, 11), (148, 12), (189, 13), (215, 14), (242, 15), (14, 16), (43, 17), (66, 18), (107, 19), (136, 20), (165, 21), (199, 22), (228, 23), (26, 24), (56, 25), (88, 26), (123, 27), (157, 28), (185, 29), (223, 30), (255, 31), (2, 32), (32, 33), (74, 34), (104, 35), (128, 36), (166, 37), (198, 38), (229, 39), (30, 40), (57, 41), (91, 42), (115, 43), (152, 44), (177, 45), (221, 46), (254, 47), (11, 48), (42, 49), (73, 50), (96, 51), (140, 52), (173, 53), (207, 54), (236, 55), (24, 56), (59, 57), (90, 58), (113, 59), (144, 60), (184, 61), (222, 62), (245, 63), (5, 64), (38, 65), (75, 66), (98, 67), (139, 68), (162, 69), (205, 70), (235, 71), (21, 72), (55, 73), (82, 74), (120, 75), (146, 76), (187, 77), (210, 78), (247, 79), (6, 80), (44, 81), (64, 82), (105, 83), (130, 84), (168, 85), (194, 86), (231, 87), (17, 88), (52, 89), (80, 90), (114, 91), (154, 92), (176, 93), (214, 94), (243, 95), (8, 96), (39, 97), (72, 98), (106, 99), (133, 100), (170, 101), (202, 102), (238, 103), (22, 104), (63, 105), (81, 106), (121, 107), (153, 108), (179, 109), (219, 110), (251, 111), (15, 112), (47, 113), (65, 114), (97, 115), (138, 116), (171, 117), (206, 118), (227, 119), (29, 120), (62, 121), (89, 122), (112, 123), (147, 124), (186, 125), (218, 126), (252, 127), (13, 128), (37, 129), (69, 130), (102, 131), (142, 132), (160, 133), (203, 134), (230, 135), (31, 136), (54, 137), (92, 138), (125, 139), (155, 140), (190, 141), (209, 142), (241, 143), (7, 144), (36, 145), (76, 146), (109, 147), (129, 148), (163, 149), (192, 150), (224, 151), (23, 152), (61, 153), (84, 154), (126, 155), (158, 156), (191, 157), (208, 158), (250, 159), (4, 160), (46, 161), (77, 162), (108, 163), (135, 164), (175, 165), (197, 166), (232, 167), (28, 168), (53, 169), (93, 170), (117, 171), (145, 172), (180, 173), (211, 174), (248, 175), (12, 176), (45, 177), (68, 178), (101, 179), (131, 180), (167, 181), (195, 182), (225, 183), (20, 184), (60, 185), (87, 186), (116, 187), (159, 188), (183, 189), (217, 190), (240, 191), (9, 192), (33, 193), (71, 194), (103, 195), (134, 196), (174, 197), (200, 198), (237, 199), (19, 200), (50, 201), (86, 202), (127, 203), (151, 204), (188, 205), (220, 206), (249, 207), (1, 208), (40, 209), (70, 210), (111, 211), (141, 212), (164, 213), (193, 214), (226, 215), (18, 216), (49, 217), (95, 218), (119, 219), (150, 220), (181, 221), (213, 222), (244, 223), (0, 224), (35, 225), (78, 226), (110, 227), (132, 228), (169, 229), (196, 230), (234, 231), (27, 232), (48, 233), (85, 234), (118, 235), (149, 236), (182, 237), (216, 238), (253, 239), (3, 240), (41, 241), (79, 242), (100, 243), (143, 244), (172, 245), (201, 246), (233, 247), (16, 248), (51, 249), (94, 250), (124, 251), (156, 252), (178, 253), (212, 254), (246, 255)]


def column_routes():
    return ROUTES


ACROSS_CORES = [(s, s ^ 1) for s in range(SECTIONS)]
SAME_CORE = [[p * C + c for p in range(PAIRS)] for c in range(C)]
SAME_PAIR = [
    [(p * C + c) * GROUPS + d for d in range(GROUPS) for c in range(C)]
    for p in range(PAIRS)
]


def terms_kernel(
    act_ref, grad_ref, in_ref, out_ref, mine_ref, theirs_ref,
    act, grad, weight_in, weight_out, low_in, low_out, sems,
):
    core = lax.rem(lax.axis_index("section"), C)
    count, length, width = act.shape
    tokens = count * length
    half = count // C
    k_out, k_in = out_ref.shape[2], in_ref.shape[3]
    group = k_out // PAIRS
    chunks = width // CHUNK

    def copies(c):
        at = pl.ds(c * CHUNK, CHUNK)
        return [
            pltpu.make_async_copy(in_ref.at[0, :, at, :], weight_in.at[:, at, :], sems.at[c, 0]),
            pltpu.make_async_copy(act_ref.at[0, :, :, at], act.at[:, :, at], sems.at[c, 1]),
            pltpu.make_async_copy(out_ref.at[0, :, :, at], weight_out.at[:, :, at], sems.at[c, 2]),
            pltpu.make_async_copy(grad_ref.at[0, :, :, at], grad.at[:, :, at], sems.at[c, 3]),
        ]

    for c in range(chunks):
        for copy in copies(c):
            copy.start()
    sum_in = sum_out = None
    for c in range(chunks):
        for copy in copies(c):
            copy.wait()
        at = slice(c * CHUNK, (c + 1) * CHUNK)
        part_in = jnp.dot(
            act[:, :, at].reshape(tokens, CHUNK),
            jnp.concatenate([weight_in[p, at, :] for p in range(PROJ)], axis=1),
            preferred_element_type=F32,
        )
        part_out = lax.dot_general(
            grad[:, :, at].reshape(tokens, CHUNK),
            weight_out[:, :, at].reshape(PROJ * k_out, CHUNK),
            (((1,), (1,)), ((), ())),
            preferred_element_type=F32,
        )
        sum_in = part_in if c == 0 else sum_in + part_in
        sum_out = part_out if c == 0 else sum_out + part_out
    low_in[...] = sum_in.astype(jnp.bfloat16)
    low_out[...] = sum_out.astype(jnp.bfloat16)
    for ref, owner in ((theirs_ref, 1 - core), (mine_ref, core)):
        for i in range(half):
            at = pl.ds(pl.multiple_of((owner * half + i) * length, length), length)
            both = lax.dot_general(
                low_out[at, :],
                low_in[at, :],
                (((0,), (0,)), ((), ())),
                preferred_element_type=F32,
            )
            term = both[:k_out, :k_in] + both[k_out:, k_in:]
            for z in range(PAIRS):
                ref[z, i * group : (i + 1) * group, :] = term[z * group : (z + 1) * group]


def layer_terms(activations, out_grads, proj_in, proj_out):
    count, length, width = activations.shape[1:]
    k_in, k_out = proj_in.shape[3], proj_out.shape[2]
    piece = jax.ShapeDtypeStruct((PAIRS, (count // C) * (k_out // PAIRS), k_in), F32)
    return pl.pallas_call(
        terms_kernel,
        in_specs=[pl.BlockSpec(memory_space=pl.ANY)] * 4,
        out_specs=[pl.BlockSpec(memory_space=pltpu.VMEM)] * 2,
        out_shape=[piece, piece],
        scratch_shapes=[
            pltpu.VMEM(activations.shape[1:], jnp.bfloat16),
            pltpu.VMEM(out_grads.shape[1:], jnp.bfloat16),
            pltpu.VMEM(proj_in.shape[1:], jnp.bfloat16),
            pltpu.VMEM(proj_out.shape[1:], jnp.bfloat16),
            pltpu.VMEM((count * length, PROJ * k_in), jnp.bfloat16),
            pltpu.VMEM((count * length, PROJ * k_out), jnp.bfloat16),
            pltpu.SemaphoreType.DMA((width // CHUNK, 4)),
        ],
        compiler_params=pltpu.CompilerParams(vmem_limit_bytes=VMEM_BYTES),
    )(activations, out_grads, proj_in, proj_out)


def gram_kernel(scale, row_ref, near_ref, far_ref, earlier_ref, gram_ref):
    core = lax.rem(lax.axis_index("section"), C)
    per_pair = 4
    examples = row_ref.shape[0] // per_pair
    rows = jnp.concatenate(
        [
            row_ref[pl.ds(core * 2 + i, examples, stride=per_pair), :]
            for i in range(2)
        ],
        axis=1,
    )
    rows = rows * scale
    for ref, owner in ((near_ref, core), (far_ref, 1 - core)):
        cols = jnp.concatenate(
            [ref[pl.ds(k, examples, stride=per_pair), :] for k in range(per_pair)],
            axis=1,
        )
        outer = lax.dot_general(
            rows,
            cols,
            (((0,), (0,)), ((), ())),
            precision=lax.Precision.HIGHEST,
            preferred_element_type=F32,
        )
        width = per_pair * LANES
        at = pl.ds(pl.multiple_of(owner * width, width), width)
        gram_ref[:, at] = earlier_ref[:, at] + outer


def add_gram(scale, rows, near, far, earlier_gram):
    return pl.pallas_call(
        functools.partial(gram_kernel, scale),
        in_specs=[pl.BlockSpec(memory_space=pltpu.VMEM)] * 4,
        out_specs=pl.BlockSpec(memory_space=pltpu.VMEM),
        out_shape=jax.ShapeDtypeStruct(earlier_gram.shape, F32),
        compiler_params=pltpu.CompilerParams(vmem_limit_bytes=16 * 2**20),
    )(rows, near, far, earlier_gram)


def per_device(activations, out_grads, proj_in, proj_out, earlier_gram):
    mine, theirs = layer_terms(activations, out_grads, proj_in, proj_out)
    mine = mine + lax.ppermute(theirs, "section", ACROSS_CORES)
    pieces = lax.all_to_all(mine, "section", 0, 0, axis_index_groups=SAME_CORE)
    reduced = pieces.sum(0)
    rows = lax.all_to_all(
        jnp.broadcast_to(reduced, (GROUPS * C, *reduced.shape)),
        BOTH,
        0,
        0,
        axis_index_groups=SAME_PAIR,
    )
    rows = rows.reshape(-1, LANES)
    near = lax.ppermute(rows, BOTH, column_routes())
    far = lax.ppermute(near, "section", ACROSS_CORES)
    total_examples = activations.shape[1] * GROUPS
    scale = 1.0 / (LEN * SECTIONS * PROJ * total_examples)
    return add_gram(scale, rows, near, far, earlier_gram)


def solution(mesh):
    return jax.shard_map(
        per_device,
        mesh=mesh,
        in_specs=(
            P("section", "dp", None, None),
            P("section", "dp", None, None),
            P("section", None, None, None),
            P("section", None, None, None),
            P("section", "dp"),
        ),
        out_specs=P("section", "dp"),
        check_vma=False,
    )
```

```python
import functools

import jax
import jax.numpy as jnp
from jax import lax
from jax.experimental import pallas as pl
from jax.experimental.pallas import tpu as pltpu
from jax.sharding import PartitionSpec as P

PROJ = 2
LEN = 64
LANES = 128
BOTH = ("section", "dp")
ZH, Y, C, ZL, X = 4, 4, 2, 2, 4
SECTIONS, GROUPS = ZH * Y * C, ZL * X
PAIRS = SECTIONS // C
CHUNK = 512
VMEM_BYTES = 53 * 2**20
F32 = jnp.float32


ACROSS_CORES = [(s, s ^ 1) for s in range(SECTIONS)]
def section_at(zh, y, c):
    return (zh * Y + y) * C + c


def shifted(by_zh, by_y):
    return [
        (section_at(zh, y, c), section_at((zh + by_zh) % ZH, (y + by_y) % Y, c))
        for zh in range(ZH)
        for y in range(Y)
        for c in range(C)
    ]


ALONG_ZH = [[section_at(zh, y, c) for zh in range(ZH)] for y in range(Y) for c in range(C)]
SAME_ZH = [
    [section_at(zh, y, c) * GROUPS + d for y in range(Y) for d in range(GROUPS)]
    for zh in range(ZH)
    for c in range(C)
]
SHARE = 3


def terms_kernel(
    act_ref, grad_ref, in_ref, out_ref, mine_ref, theirs_ref,
    act, grad, weight_in, weight_out, low_in, low_out, term, sems,
):
    section = lax.axis_index("section")
    core = lax.rem(section, C)
    y = lax.rem(lax.div(section, C), Y)
    count, length, width = act.shape
    tokens = count * length
    half = count // C
    k_out, k_in = out_ref.shape[2], in_ref.shape[3]
    group = k_out // PAIRS
    chunks = width // CHUNK

    def copies(c):
        at = pl.ds(c * CHUNK, CHUNK)
        return [
            pltpu.make_async_copy(in_ref.at[0, :, at, :], weight_in.at[:, at, :], sems.at[c, 0]),
            pltpu.make_async_copy(act_ref.at[0, :, :, at], act.at[:, :, at], sems.at[c, 1]),
            pltpu.make_async_copy(out_ref.at[0, :, :, at], weight_out.at[:, :, at], sems.at[c, 2]),
            pltpu.make_async_copy(grad_ref.at[0, :, :, at], grad.at[:, :, at], sems.at[c, 3]),
        ]

    for c in range(chunks):
        for copy in copies(c):
            copy.start()
    sum_in = sum_out = None
    for c in range(chunks):
        for copy in copies(c):
            copy.wait()
        at = slice(c * CHUNK, (c + 1) * CHUNK)
        part_in = jnp.dot(
            act[:, :, at].reshape(tokens, CHUNK),
            jnp.concatenate([weight_in[p, at, :] for p in range(PROJ)], axis=1),
            preferred_element_type=F32,
        )
        part_out = lax.dot_general(
            grad[:, :, at].reshape(tokens, CHUNK),
            weight_out[:, :, at].reshape(PROJ * k_out, CHUNK),
            (((1,), (1,)), ((), ())),
            preferred_element_type=F32,
        )
        sum_in = part_in if c == 0 else sum_in + part_in
        sum_out = part_out if c == 0 else sum_out + part_out
    low_in[...] = sum_in.astype(jnp.bfloat16)
    low_out[...] = sum_out.astype(jnp.bfloat16)
    for ref, owner in ((theirs_ref, 1 - core), (mine_ref, core)):
        for i in range(half):
            at = pl.ds(pl.multiple_of((owner * half + i) * length, length), length)
            both = lax.dot_general(
                low_out[at, :],
                low_in[at, :],
                (((0,), (0,)), ((), ())),
                preferred_element_type=F32,
            )
            term[...] = both[:k_out, :k_in] + both[k_out:, k_in:]
            for k in range(group):
                ref[lax.rem(k - y + Y, Y), pl.ds(i, PAIRS, stride=half), :] = term[
                    pl.ds(k, PAIRS, stride=group), :
                ]


def layer_terms(activations, out_grads, proj_in, proj_out):
    count, length, width = activations.shape[1:]
    k_in, k_out = proj_in.shape[3], proj_out.shape[2]
    piece = jax.ShapeDtypeStruct((k_out // PAIRS, PAIRS * (count // C), k_in), F32)
    return pl.pallas_call(
        terms_kernel,
        in_specs=[pl.BlockSpec(memory_space=pl.ANY)] * 4,
        out_specs=[pl.BlockSpec(memory_space=pltpu.VMEM)] * 2,
        out_shape=[piece, piece],
        scratch_shapes=[
            pltpu.VMEM(activations.shape[1:], jnp.bfloat16),
            pltpu.VMEM(out_grads.shape[1:], jnp.bfloat16),
            pltpu.VMEM(proj_in.shape[1:], jnp.bfloat16),
            pltpu.VMEM(proj_out.shape[1:], jnp.bfloat16),
            pltpu.VMEM((count * length, PROJ * k_in), jnp.bfloat16),
            pltpu.VMEM((count * length, PROJ * k_out), jnp.bfloat16),
            pltpu.VMEM((k_out, k_in), F32),
            pltpu.SemaphoreType.DMA((width // CHUNK, 4)),
        ],
        compiler_params=pltpu.CompilerParams(vmem_limit_bytes=VMEM_BYTES),
    )(activations, out_grads, proj_in, proj_out)


def thirds(value):
    parts = []
    for _ in range(3):
        part = value.astype(jnp.bfloat16)
        parts.append(part)
        value = value - part.astype(F32)
    return parts


def pack_kernel(ref_0, ref_1, ref_2, ref_3, packed_ref, reduced):
    zh = lax.div(lax.axis_index("section"), Y * C)
    reduced[...] = (ref_0[...] + ref_1[...]) + (ref_2[...] + ref_3[...])
    half = reduced.shape[0] // PAIRS
    for y in range(Y):
        row = reduced[pl.ds(pl.multiple_of((zh * Y + y) * half, half), half), :]
        for d in range(GROUPS):
            at = (y * GROUPS + d) * SHARE * half
            packed_ref[at : at + half, :] = row
            packed_ref[at + half : at + SHARE * half, :] = reduced[
                d * 2 * half : (d + 1) * 2 * half, :
            ]


def pack(pieces):
    shape = pieces[0].shape
    return pl.pallas_call(
        pack_kernel,
        in_specs=[pl.BlockSpec(memory_space=pltpu.VMEM)] * ZH,
        out_specs=pl.BlockSpec(memory_space=pltpu.VMEM),
        out_shape=jax.ShapeDtypeStruct(
            (Y * GROUPS * SHARE * (shape[0] // PAIRS), shape[1]), F32
        ),
        scratch_shapes=[pltpu.VMEM(shape, F32)],
        compiler_params=pltpu.CompilerParams(vmem_limit_bytes=8 * 2**20),
    )(*pieces)


def gathered(ref, k, row):
    half = ref.shape[0] // (Y * GROUPS * SHARE)
    return jnp.concatenate(
        [
            ref[pl.ds((k * GROUPS * SHARE + row) * half + e, GROUPS, stride=SHARE * half), :]
            for e in range(half)
        ],
        axis=0,
    )


def outer_product(ref, core, scale):
    r = thirds(
        jnp.concatenate([gathered(ref, core * 2 + k, 0) for k in range(2)], axis=1) * scale
    )
    c = thirds(
        jnp.concatenate([gathered(ref, k, 1 + j) for j in range(2) for k in range(4)], axis=1)
    )
    pairs = [(0, 0), (0, 1), (1, 0), (1, 1), (0, 2), (2, 0)]
    return lax.dot_general(
        jnp.concatenate([r[i] for i, _ in pairs], axis=0),
        jnp.concatenate([c[j] for _, j in pairs], axis=0),
        (((0,), (0,)), ((), ())),
        preferred_element_type=F32,
    )


def gram_kernel(scale, ref, earlier_ref, gram_ref):
    core = lax.rem(lax.axis_index("section"), C)
    gram_ref[...] = earlier_ref[...] + outer_product(ref, core, scale)


def add_gram(scale, features, earlier_gram):
    shape = earlier_gram.shape
    return pl.pallas_call(
        functools.partial(gram_kernel, scale),
        in_specs=[pl.BlockSpec(memory_space=pltpu.VMEM)] * 2,
        out_specs=pl.BlockSpec(memory_space=pltpu.VMEM),
        out_shape=jax.ShapeDtypeStruct(shape, F32),
        cost_estimate=pl.CostEstimate(
            flops=12 * shape[0] * shape[1] * 32,
            bytes_accessed=4 * shape[0] * shape[1],
            transcendentals=0,
        ),
        compiler_params=pltpu.CompilerParams(vmem_limit_bytes=16 * 2**20),
    )(features, earlier_gram)


def per_device(activations, out_grads, proj_in, proj_out, earlier_gram):
    mine, theirs = layer_terms(activations, out_grads, proj_in, proj_out)
    mine = mine + lax.ppermute(theirs, "section", ACROSS_CORES)
    reduced = mine[0]
    for turn in (2, 1, 3):
        reduced = reduced + lax.ppermute(mine[turn], "section", shifted(0, turn))
    pieces = [reduced] + [
        lax.ppermute(reduced, "section", shifted(turn, 0)) for turn in (2, 1, 3)
    ]
    packed = pack(pieces)
    rows = packed.shape[0] // (Y * GROUPS * SHARE)
    packed = packed.reshape(Y * GROUPS, SHARE, rows, LANES)
    near = lax.all_to_all(packed, BOTH, 0, 0, axis_index_groups=SAME_ZH)
    near = near.reshape(-1, LANES)
    far = lax.ppermute(near, "section", ACROSS_CORES)
    total_examples = activations.shape[1] * GROUPS
    scale = 1.0 / (LEN * SECTIONS * PROJ * total_examples)
    return add_gram(scale, far, add_gram(scale, near, earlier_gram))


def solution(mesh):
    return jax.shard_map(
        per_device,
        mesh=mesh,
        in_specs=(
            P("section", "dp", None, None),
            P("section", "dp", None, None),
            P("section", None, None, None),
            P("section", None, None, None),
            P("section", "dp"),
        ),
        out_specs=P("section", "dp"),
        check_vma=False,
    )
```

```python
import functools

import jax
import jax.numpy as jnp
from jax import lax
from jax.experimental import pallas as pl
from jax.experimental.pallas import tpu as pltpu
from jax.sharding import PartitionSpec as P

PROJ = 2
LEN = 64
LANES = 128
BOTH = ("section", "dp")
ZH, Y, C, ZL, X = 4, 4, 2, 2, 4
SECTIONS, GROUPS = ZH * Y * C, ZL * X
PAIRS = SECTIONS // C
CHUNKS = (256, 768, 1024, 1024, 512, 512)
VMEM_BYTES = 24 * 2**20
F32 = jnp.float32


ACROSS_CORES = [(s, s ^ 1) for s in range(SECTIONS)]
def section_at(zh, y, c):
    return (zh * Y + y) * C + c


def across(by_zh, by_y):
    return [
        (section_at(zh, y, c), section_at(zh ^ by_zh, y ^ by_y, c))
        for zh in range(ZH)
        for y in range(Y)
        for c in range(C)
    ]


SAME_ZH = [
    [section_at(zh, y, c) * GROUPS + d for y in range(Y) for d in range(GROUPS)]
    for zh in range(ZH)
    for c in range(C)
]
SHARE = 3
OUT_PARTS = 2


def project(act, grad, weight_in, weight_out, first, size):
    at = slice(first, first + size)
    tokens = act.shape[0] * act.shape[1]
    k_out = weight_out.shape[1]
    return (
        jnp.dot(
            act[:, :, at].reshape(tokens, size),
            jnp.concatenate([weight_in[p, at, :] for p in range(PROJ)], axis=1),
            preferred_element_type=F32,
        ),
        lax.dot_general(
            grad[:, :, at].reshape(tokens, size),
            weight_out[:, :, at].reshape(PROJ * k_out, size),
            (((1,), (1,)), ((), ())),
            preferred_element_type=F32,
        ),
    )


def write_terms(sums, ref, term):
    y = lax.rem(lax.div(lax.axis_index("section"), C), Y)
    count, k_out, k_in = term.shape
    length = sums[0].shape[0] // count
    group = k_out // PAIRS
    low_in, low_out = (part.astype(jnp.bfloat16) for part in sums)
    for i in range(count):
        tokens = slice(i * length, (i + 1) * length)
        both = lax.dot_general(
            low_out[tokens],
            low_in[tokens],
            (((0,), (0,)), ((), ())),
            preferred_element_type=F32,
        )
        term[i] = both[:k_out, :k_in] + both[k_out:, k_in:]
        for k in range(group):
            ref[lax.bitwise_xor(y, k), pl.ds(i, PAIRS, stride=count), :] = term[
                i, pl.ds(k, PAIRS, stride=group), :
            ]


def theirs_kernel(
    act_ref, grad_ref, in_ref, out_ref,
    theirs_ref, act_mine, grad_mine, weight_in, weight_out,
    act, grad, term, sems, mine_sems,
):
    core = lax.rem(lax.axis_index("section"), C)
    half = act.shape[0]
    theirs, mine = pl.ds((1 - core) * half, half), pl.ds(core * half, half)
    spans = [(sum(CHUNKS[:c]), size) for c, size in enumerate(CHUNKS)]

    def copies(c):
        at = pl.ds(*spans[c])
        return [
            pltpu.make_async_copy(in_ref.at[0, :, at, :], weight_in.at[:, at, :], sems.at[c, 0]),
            pltpu.make_async_copy(act_ref.at[0, theirs, :, at], act.at[:, :, at], sems.at[c, 1]),
            pltpu.make_async_copy(out_ref.at[0, :, :, at], weight_out.at[:, :, at], sems.at[c, 2]),
            pltpu.make_async_copy(grad_ref.at[0, theirs, :, at], grad.at[:, :, at], sems.at[c, 3]),
        ]

    later = [
        pltpu.make_async_copy(act_ref.at[0, mine], act_mine, mine_sems.at[0]),
        pltpu.make_async_copy(grad_ref.at[0, mine], grad_mine, mine_sems.at[1]),
    ]
    for c in range(len(spans)):
        for copy in copies(c):
            copy.start()
    for copy in later:
        copy.start()
    sums = None
    for c in range(len(spans)):
        for copy in copies(c):
            copy.wait()
        parts = project(act, grad, weight_in, weight_out, *spans[c])
        sums = parts if sums is None else [s + p for s, p in zip(sums, parts)]
    write_terms(sums, theirs_ref, term)
    for copy in later:
        copy.wait()


def mine_kernel(act, grad, weight_in, weight_out, mine_ref, term):
    sums = None
    size = 1024
    for first in range(0, act.shape[2], size):
        parts = project(act, grad, weight_in, weight_out, first, size)
        sums = parts if sums is None else [s + p for s, p in zip(sums, parts)]
    write_terms(sums, mine_ref, term)


def layer_terms(activations, out_grads, proj_in, proj_out):
    count, length, width = activations.shape[1:]
    half = count // C
    k_in, k_out = proj_in.shape[3], proj_out.shape[2]
    piece = jax.ShapeDtypeStruct((k_out // PAIRS, PAIRS * half, k_in), F32)
    tokens = jax.ShapeDtypeStruct((half, length, width), jnp.bfloat16)
    vmem = pl.BlockSpec(memory_space=pltpu.VMEM)
    theirs, *kept = pl.pallas_call(
        theirs_kernel,
        in_specs=[pl.BlockSpec(memory_space=pl.ANY)] * 4,
        out_specs=[vmem] * 5,
        out_shape=[
            piece,
            tokens,
            tokens,
            jax.ShapeDtypeStruct(proj_in.shape[1:], jnp.bfloat16),
            jax.ShapeDtypeStruct(proj_out.shape[1:], jnp.bfloat16),
        ],
        scratch_shapes=[
            pltpu.VMEM(tokens.shape, jnp.bfloat16),
            pltpu.VMEM(tokens.shape, jnp.bfloat16),
            pltpu.VMEM((half, k_out, k_in), F32),
            pltpu.SemaphoreType.DMA((len(CHUNKS), 4)),
            pltpu.SemaphoreType.DMA((2,)),
        ],
        compiler_params=pltpu.CompilerParams(vmem_limit_bytes=VMEM_BYTES),
    )(*(pltpu.with_memory_space_constraint(a, pltpu.HBM) for a in (activations, out_grads, proj_in, proj_out)))
    mine = pl.pallas_call(
        mine_kernel,
        in_specs=[vmem] * 4,
        out_specs=vmem,
        out_shape=piece,
        scratch_shapes=[pltpu.VMEM((half, k_out, k_in), F32)],
        cost_estimate=pl.CostEstimate(
            flops=2 * half * length * width * PROJ * (k_in + k_out),
            bytes_accessed=8 * 2**20,
            transcendentals=0,
        ),
        compiler_params=pltpu.CompilerParams(vmem_limit_bytes=16 * 2**20),
    )(*kept)
    return mine, theirs


def thirds(value):
    parts = []
    for _ in range(3):
        part = value.astype(jnp.bfloat16)
        parts.append(part)
        value = value - part.astype(F32)
    return parts


def pack_kernel(ref_0, ref_1, ref_2, ref_3, packed_ref, reduced):
    zh = lax.div(lax.axis_index("section"), Y * C)
    reduced[...] = (ref_0[...] + ref_1[...]) + (ref_2[...] + ref_3[...])
    half = reduced.shape[0] // PAIRS
    for y in range(Y):
        row = reduced[pl.ds(pl.multiple_of((zh * Y + y) * half, half), half), :]
        for d in range(GROUPS):
            at = (y * GROUPS + d) * SHARE * half
            packed_ref[at : at + half, :] = row
            packed_ref[at + half : at + SHARE * half, :] = reduced[
                d * 2 * half : (d + 1) * 2 * half, :
            ]


def pack(pieces):
    shape = pieces[0].shape
    return pl.pallas_call(
        pack_kernel,
        in_specs=[pl.BlockSpec(memory_space=pltpu.VMEM)] * ZH,
        out_specs=pl.BlockSpec(memory_space=pltpu.VMEM),
        out_shape=jax.ShapeDtypeStruct(
            (Y * GROUPS * SHARE * (shape[0] // PAIRS), shape[1]), F32
        ),
        scratch_shapes=[pltpu.VMEM(shape, F32)],
        compiler_params=pltpu.CompilerParams(vmem_limit_bytes=8 * 2**20),
    )(*pieces)


def gathered(ref, k, row):
    half = ref.shape[0] // (Y * GROUPS * SHARE)
    return jnp.concatenate(
        [
            ref[pl.ds((k * GROUPS * SHARE + row) * half + e, GROUPS, stride=SHARE * half), :]
            for e in range(half)
        ],
        axis=0,
    )


def factors(ref, core, scale):
    r = thirds(
        jnp.concatenate([gathered(ref, core * 2 + k, 0) for k in range(2)], axis=1) * scale
    )
    c = thirds(
        jnp.concatenate([gathered(ref, k, 1 + j) for j in range(2) for k in range(4)], axis=1)
    )
    pairs = [(0, 0), (0, 1), (1, 0), (1, 1), (0, 2), (2, 0)]
    return (
        jnp.concatenate([r[i] for i, _ in pairs], axis=0),
        jnp.concatenate([c[j] for _, j in pairs], axis=0),
    )


def outer_product(ref, core, scale):
    rows, cols = factors(ref, core, scale)
    return lax.dot_general(
        rows, cols, (((0,), (0,)), ((), ())), preferred_element_type=F32
    )


def near_kernel(scale, ref, earlier_ref, held_ref):
    core = lax.rem(lax.axis_index("section"), C)
    held_ref[...] = earlier_ref[...] + outer_product(ref, core, scale)


def far_kernel(scale, ref, held_ref, gram_ref, total, sems):
    core = lax.rem(lax.axis_index("section"), C)
    rows, cols = factors(ref, core, scale)
    count = sems.shape[0]
    size = total.shape[0] // count
    copies = []
    for i in range(count):
        at = slice(i * size, (i + 1) * size)
        total[at, :] = held_ref[at, :] + lax.dot_general(
            rows[:, at], cols, (((0,), (0,)), ((), ())), preferred_element_type=F32
        )
        copy = pltpu.make_async_copy(total.at[at, :], gram_ref.at[at, :], sems.at[i])
        copy.start()
        copies.append(copy)
    for copy in copies:
        copy.wait()


def add_near(scale, features, earlier_gram):
    shape = earlier_gram.shape
    return pl.pallas_call(
        functools.partial(near_kernel, scale),
        in_specs=[pl.BlockSpec(memory_space=pltpu.VMEM)] * 2,
        out_specs=pl.BlockSpec(memory_space=pltpu.VMEM),
        out_shape=jax.ShapeDtypeStruct(shape, F32),
        cost_estimate=pl.CostEstimate(
            flops=12 * shape[0] * shape[1] * 32,
            bytes_accessed=4 * shape[0] * shape[1],
            transcendentals=0,
        ),
        compiler_params=pltpu.CompilerParams(vmem_limit_bytes=16 * 2**20),
    )(features, earlier_gram)


def add_far(scale, features, held):
    return pl.pallas_call(
        functools.partial(far_kernel, scale),
        in_specs=[pl.BlockSpec(memory_space=pltpu.VMEM)] * 2,
        out_specs=pl.BlockSpec(memory_space=pl.ANY),
        out_shape=jax.ShapeDtypeStruct(held.shape, F32),
        scratch_shapes=[
            pltpu.VMEM(held.shape, F32),
            pltpu.SemaphoreType.DMA((OUT_PARTS,)),
        ],
        compiler_params=pltpu.CompilerParams(vmem_limit_bytes=16 * 2**20),
    )(features, held)


def per_device(activations, out_grads, proj_in, proj_out, earlier_gram):
    mine, theirs = layer_terms(activations, out_grads, proj_in, proj_out)
    mine = mine + lax.ppermute(theirs, "section", ACROSS_CORES)
    reduced = mine[0]
    for turn in (2, 1, 3):
        reduced = reduced + lax.ppermute(mine[turn], "section", across(0, turn))
    pieces = [reduced] + [
        lax.ppermute(reduced, "section", across(turn, 0)) for turn in (1, 3, 2)
    ]
    packed = pack(pieces)
    rows = packed.shape[0] // (Y * GROUPS * SHARE)
    packed = packed.reshape(Y * GROUPS, SHARE, rows, LANES)
    near = lax.all_to_all(packed, BOTH, 0, 0, axis_index_groups=SAME_ZH)
    near = near.reshape(-1, LANES)
    far = lax.ppermute(near, "section", ACROSS_CORES)
    total_examples = activations.shape[1] * GROUPS
    scale = 1.0 / (LEN * SECTIONS * PROJ * total_examples)
    return add_far(scale, far, add_near(scale, near, earlier_gram))


def solution(mesh):
    return jax.shard_map(
        per_device,
        mesh=mesh,
        in_specs=(
            P("section", "dp", None, None),
            P("section", "dp", None, None),
            P("section", None, None, None),
            P("section", None, None, None),
            P("section", "dp"),
        ),
        out_specs=P("section", "dp"),
        check_vma=False,
    )
```

```python
import functools

import jax
import jax.numpy as jnp
from jax import lax
from jax.experimental import pallas as pl
from jax.experimental.pallas import tpu as pltpu
from jax.sharding import PartitionSpec as P

PROJ = 2
LEN = 64
LANES = 128
BOTH = ("section", "dp")
ZH, Y, C, ZL, X = 4, 4, 2, 2, 4
SECTIONS, GROUPS = ZH * Y * C, ZL * X
PAIRS = SECTIONS // C
CHUNKS = (256, 768, 1024, 1024, 512, 512)
VMEM_BYTES = 24 * 2**20
F32 = jnp.float32


ACROSS_CORES = [(s, s ^ 1) for s in range(SECTIONS)]
def section_at(zh, y, c):
    return (zh * Y + y) * C + c


def across(by_zh, by_y):
    return [
        (section_at(zh, y, c), section_at(zh ^ by_zh, y ^ by_y, c))
        for zh in range(ZH)
        for y in range(Y)
        for c in range(C)
    ]


SAME_ZH = [
    [section_at(zh, y, c) * GROUPS + d for y in reversed(range(Y)) for d in reversed(range(GROUPS))]
    for zh in range(ZH)
    for c in range(C)
]
SHARE = 3
OUT_PARTS = 2


def project(act, grad, weight_in, weight_out, first, size):
    at = slice(first, first + size)
    tokens = act.shape[0] * act.shape[1]
    k_out = weight_out.shape[1]
    return (
        jnp.dot(
            act[:, :, at].reshape(tokens, size),
            jnp.concatenate([weight_in[p, at, :] for p in range(PROJ)], axis=1),
            preferred_element_type=F32,
        ),
        lax.dot_general(
            grad[:, :, at].reshape(tokens, size),
            weight_out[:, :, at].reshape(PROJ * k_out, size),
            (((1,), (1,)), ((), ())),
            preferred_element_type=F32,
        ),
    )


def write_terms(sums, ref, term):
    y = lax.rem(lax.div(lax.axis_index("section"), C), Y)
    count, k_out, k_in = term.shape
    length = sums[0].shape[0] // count
    group = k_out // PAIRS
    low_in, low_out = (part.astype(jnp.bfloat16) for part in sums)
    for i in range(count):
        tokens = slice(i * length, (i + 1) * length)
        both = lax.dot_general(
            low_out[tokens],
            low_in[tokens],
            (((0,), (0,)), ((), ())),
            preferred_element_type=F32,
        )
        term[i] = both[:k_out, :k_in] + both[k_out:, k_in:]
        for k in range(group):
            ref[lax.bitwise_xor(y, k), pl.ds(i, PAIRS, stride=count), :] = term[
                i, pl.ds(k, PAIRS, stride=group), :
            ]


def theirs_kernel(
    act_ref, grad_ref, in_ref, out_ref,
    theirs_ref, act_mine, grad_mine, weight_in, weight_out,
    act, grad, term, sems, mine_sems,
):
    core = lax.rem(lax.axis_index("section"), C)
    half = act.shape[0]
    theirs, mine = pl.ds((1 - core) * half, half), pl.ds(core * half, half)
    spans = [(sum(CHUNKS[:c]), size) for c, size in enumerate(CHUNKS)]

    def copies(c):
        at = pl.ds(*spans[c])
        return [
            pltpu.make_async_copy(in_ref.at[0, :, at, :], weight_in.at[:, at, :], sems.at[c, 0]),
            pltpu.make_async_copy(act_ref.at[0, theirs, :, at], act.at[:, :, at], sems.at[c, 1]),
            pltpu.make_async_copy(out_ref.at[0, :, :, at], weight_out.at[:, :, at], sems.at[c, 2]),
            pltpu.make_async_copy(grad_ref.at[0, theirs, :, at], grad.at[:, :, at], sems.at[c, 3]),
        ]

    later = [
        pltpu.make_async_copy(act_ref.at[0, mine], act_mine, mine_sems.at[0]),
        pltpu.make_async_copy(grad_ref.at[0, mine], grad_mine, mine_sems.at[1]),
    ]
    for c in range(len(spans)):
        for copy in copies(c):
            copy.start()
    for copy in later:
        copy.start()
    sums = None
    for c in range(len(spans)):
        for copy in copies(c):
            copy.wait()
        parts = project(act, grad, weight_in, weight_out, *spans[c])
        sums = parts if sums is None else [s + p for s, p in zip(sums, parts)]
    write_terms(sums, theirs_ref, term)
    for copy in later:
        copy.wait()


def mine_kernel(act, grad, weight_in, weight_out, mine_ref, term):
    sums = None
    size = 1024
    for first in range(0, act.shape[2], size):
        parts = project(act, grad, weight_in, weight_out, first, size)
        sums = parts if sums is None else [s + p for s, p in zip(sums, parts)]
    write_terms(sums, mine_ref, term)


def layer_terms(activations, out_grads, proj_in, proj_out):
    count, length, width = activations.shape[1:]
    half = count // C
    k_in, k_out = proj_in.shape[3], proj_out.shape[2]
    piece = jax.ShapeDtypeStruct((k_out // PAIRS, PAIRS * half, k_in), F32)
    tokens = jax.ShapeDtypeStruct((half, length, width), jnp.bfloat16)
    vmem = pl.BlockSpec(memory_space=pltpu.VMEM)
    theirs, *kept = pl.pallas_call(
        theirs_kernel,
        in_specs=[pl.BlockSpec(memory_space=pl.ANY)] * 4,
        out_specs=[vmem] * 5,
        out_shape=[
            piece,
            tokens,
            tokens,
            jax.ShapeDtypeStruct(proj_in.shape[1:], jnp.bfloat16),
            jax.ShapeDtypeStruct(proj_out.shape[1:], jnp.bfloat16),
        ],
        scratch_shapes=[
            pltpu.VMEM(tokens.shape, jnp.bfloat16),
            pltpu.VMEM(tokens.shape, jnp.bfloat16),
            pltpu.VMEM((half, k_out, k_in), F32),
            pltpu.SemaphoreType.DMA((len(CHUNKS), 4)),
            pltpu.SemaphoreType.DMA((2,)),
        ],
        compiler_params=pltpu.CompilerParams(vmem_limit_bytes=VMEM_BYTES),
    )(*(pltpu.with_memory_space_constraint(a, pltpu.HBM) for a in (activations, out_grads, proj_in, proj_out)))
    mine = pl.pallas_call(
        mine_kernel,
        in_specs=[vmem] * 4,
        out_specs=vmem,
        out_shape=piece,
        scratch_shapes=[pltpu.VMEM((half, k_out, k_in), F32)],
        cost_estimate=pl.CostEstimate(
            flops=2 * half * length * width * PROJ * (k_in + k_out),
            bytes_accessed=8 * 2**20,
            transcendentals=0,
        ),
        compiler_params=pltpu.CompilerParams(vmem_limit_bytes=16 * 2**20),
    )(*kept)
    return mine, theirs


def thirds(value):
    parts = []
    for _ in range(3):
        part = value.astype(jnp.bfloat16)
        parts.append(part)
        value = value - part.astype(F32)
    return parts


def pack_kernel(ref_0, ref_1, ref_2, ref_3, packed_ref, reduced):
    zh = lax.div(lax.axis_index("section"), Y * C)
    reduced[...] = (ref_0[...] + ref_1[...]) + (ref_2[...] + ref_3[...])
    half = reduced.shape[0] // PAIRS
    for y in range(Y):
        row = reduced[pl.ds(pl.multiple_of((zh * Y + y) * half, half), half), :]
        for d in range(GROUPS):
            at = ((Y - 1 - y) * GROUPS + GROUPS - 1 - d) * SHARE * half
            packed_ref[at : at + half, :] = row
            packed_ref[at + half : at + SHARE * half, :] = reduced[
                d * 2 * half : (d + 1) * 2 * half, :
            ]


def pack(pieces):
    shape = pieces[0].shape
    return pl.pallas_call(
        pack_kernel,
        in_specs=[pl.BlockSpec(memory_space=pltpu.VMEM)] * ZH,
        out_specs=pl.BlockSpec(memory_space=pltpu.VMEM),
        out_shape=jax.ShapeDtypeStruct(
            (Y * GROUPS * SHARE * (shape[0] // PAIRS), shape[1]), F32
        ),
        scratch_shapes=[pltpu.VMEM(shape, F32)],
        compiler_params=pltpu.CompilerParams(vmem_limit_bytes=8 * 2**20),
    )(*pieces)


def gathered(ref, k, row):
    half = ref.shape[0] // (Y * GROUPS * SHARE)
    return jnp.concatenate(
        [
            ref[pl.ds(((Y - 1 - k) * GROUPS * SHARE + row) * half + e, GROUPS, stride=SHARE * half), :]
            for e in range(half)
        ],
        axis=0,
    )


def factors(ref, core, scale):
    r = thirds(
        jnp.concatenate([gathered(ref, core * 2 + k, 0) for k in range(2)], axis=1) * scale
    )
    c = thirds(
        jnp.concatenate([gathered(ref, k, 1 + j) for j in range(2) for k in range(4)], axis=1)
    )
    pairs = [(0, 0), (0, 1), (1, 0), (1, 1), (0, 2), (2, 0)]
    return (
        jnp.concatenate([r[i] for i, _ in pairs], axis=0),
        jnp.concatenate([c[j] for _, j in pairs], axis=0),
    )


def outer_product(ref, core, scale):
    rows, cols = factors(ref, core, scale)
    return lax.dot_general(
        rows, cols, (((0,), (0,)), ((), ())), preferred_element_type=F32
    )


def near_kernel(scale, ref, earlier_ref, held_ref):
    core = lax.rem(lax.axis_index("section"), C)
    held_ref[...] = earlier_ref[...] + outer_product(ref, core, scale)


def far_kernel(scale, ref, held_ref, gram_ref, total, sems):
    core = lax.rem(lax.axis_index("section"), C)
    rows, cols = factors(ref, core, scale)
    count = sems.shape[0]
    size = total.shape[0] // count
    copies = []
    for i in range(count):
        at = slice(i * size, (i + 1) * size)
        total[at, :] = held_ref[at, :] + lax.dot_general(
            rows[:, at], cols, (((0,), (0,)), ((), ())), preferred_element_type=F32
        )
        copy = pltpu.make_async_copy(total.at[at, :], gram_ref.at[at, :], sems.at[i])
        copy.start()
        copies.append(copy)
    for copy in copies:
        copy.wait()


def add_near(scale, features, earlier_gram):
    shape = earlier_gram.shape
    return pl.pallas_call(
        functools.partial(near_kernel, scale),
        in_specs=[pl.BlockSpec(memory_space=pltpu.VMEM)] * 2,
        out_specs=pl.BlockSpec(memory_space=pltpu.VMEM),
        out_shape=jax.ShapeDtypeStruct(shape, F32),
        cost_estimate=pl.CostEstimate(
            flops=12 * shape[0] * shape[1] * 32,
            bytes_accessed=4 * shape[0] * shape[1],
            transcendentals=0,
        ),
        compiler_params=pltpu.CompilerParams(vmem_limit_bytes=16 * 2**20),
    )(features, earlier_gram)


def add_far(scale, features, held):
    return pl.pallas_call(
        functools.partial(far_kernel, scale),
        in_specs=[pl.BlockSpec(memory_space=pltpu.VMEM)] * 2,
        out_specs=pl.BlockSpec(memory_space=pl.ANY),
        out_shape=jax.ShapeDtypeStruct(held.shape, F32),
        scratch_shapes=[
            pltpu.VMEM(held.shape, F32),
            pltpu.SemaphoreType.DMA((OUT_PARTS,)),
        ],
        compiler_params=pltpu.CompilerParams(vmem_limit_bytes=16 * 2**20),
    )(features, held)


def per_device(activations, out_grads, proj_in, proj_out, earlier_gram):
    mine, theirs = layer_terms(activations, out_grads, proj_in, proj_out)
    mine = mine + lax.ppermute(theirs, "section", ACROSS_CORES)
    reduced = mine[0]
    for turn in (2, 1, 3):
        reduced = reduced + lax.ppermute(mine[turn], "section", across(0, turn))
    pieces = [reduced] + [
        lax.ppermute(reduced, "section", across(turn, 0)) for turn in (1, 3, 2)
    ]
    packed = pack(pieces)
    rows = packed.shape[0] // (Y * GROUPS * SHARE)
    packed = packed.reshape(Y * GROUPS, SHARE, rows, LANES)
    near = lax.all_to_all(packed, BOTH, 0, 0, axis_index_groups=SAME_ZH)
    near = near.reshape(-1, LANES)
    far = lax.ppermute(near, "section", ACROSS_CORES)
    total_examples = activations.shape[1] * GROUPS
    scale = 1.0 / (LEN * SECTIONS * PROJ * total_examples)
    return add_far(scale, far, add_near(scale, near, earlier_gram))


def solution(mesh):
    return jax.shard_map(
        per_device,
        mesh=mesh,
        in_specs=(
            P("section", "dp", None, None),
            P("section", "dp", None, None),
            P("section", None, None, None),
            P("section", None, None, None),
            P("section", "dp"),
        ),
        out_specs=P("section", "dp"),
        check_vma=False,
    )
```

```python
import functools

import jax
import jax.numpy as jnp
from jax import lax
from jax.experimental import pallas as pl
from jax.experimental.pallas import tpu as pltpu
from jax.sharding import PartitionSpec as P

PROJ = 2
LEN = 64
LANES = 128
BOTH = ("section", "dp")
ZH, Y, C, ZL, X = 4, 4, 2, 2, 4
SECTIONS, GROUPS = ZH * Y * C, ZL * X
PAIRS = SECTIONS // C
CHUNKS = (256, 768, 1024, 1024, 512, 512)
VMEM_BYTES = 24 * 2**20
F32 = jnp.float32


ACROSS_CORES = [(s, s ^ 1) for s in range(SECTIONS)]
def section_at(zh, y, c):
    return (zh * Y + y) * C + c


def across(by_zh, by_y):
    return [
        (section_at(zh, y, c), section_at(zh ^ by_zh, y ^ by_y, c))
        for zh in range(ZH)
        for y in range(Y)
        for c in range(C)
    ]


Y_RANKS = (2, 3, 1, 0)
D_RANKS = (7, 6, 5, 4, 3, 2, 1, 0)
SAME_ZH = [
    [section_at(zh, y, c) * GROUPS + d for y in Y_RANKS for d in D_RANKS]
    for zh in range(ZH)
    for c in range(C)
]
SHARE = 3
OUT_PARTS = 2


def project(act, grad, weight_in, weight_out, first, size):
    at = slice(first, first + size)
    tokens = act.shape[0] * act.shape[1]
    k_out = weight_out.shape[1]
    return (
        jnp.dot(
            act[:, :, at].reshape(tokens, size),
            jnp.concatenate([weight_in[p, at, :] for p in range(PROJ)], axis=1),
            preferred_element_type=F32,
        ),
        lax.dot_general(
            grad[:, :, at].reshape(tokens, size),
            weight_out[:, :, at].reshape(PROJ * k_out, size),
            (((1,), (1,)), ((), ())),
            preferred_element_type=F32,
        ),
    )


def write_terms(sums, ref, term):
    y = lax.rem(lax.div(lax.axis_index("section"), C), Y)
    count, k_out, k_in = term.shape
    length = sums[0].shape[0] // count
    group = k_out // PAIRS
    low_in, low_out = (part.astype(jnp.bfloat16) for part in sums)
    for i in range(count):
        tokens = slice(i * length, (i + 1) * length)
        both = lax.dot_general(
            low_out[tokens],
            low_in[tokens],
            (((0,), (0,)), ((), ())),
            preferred_element_type=F32,
        )
        term[i] = both[:k_out, :k_in] + both[k_out:, k_in:]
        for k in range(group):
            ref[lax.bitwise_xor(y, k), pl.ds(i, PAIRS, stride=count), :] = term[
                i, pl.ds(k, PAIRS, stride=group), :
            ]


def theirs_kernel(
    act_ref, grad_ref, in_ref, out_ref,
    theirs_ref, act_mine, grad_mine, weight_in, weight_out,
    act, grad, term, sems, mine_sems,
):
    core = lax.rem(lax.axis_index("section"), C)
    half = act.shape[0]
    theirs, mine = pl.ds((1 - core) * half, half), pl.ds(core * half, half)
    spans = [(sum(CHUNKS[:c]), size) for c, size in enumerate(CHUNKS)]

    def copies(c):
        at = pl.ds(*spans[c])
        return [
            pltpu.make_async_copy(in_ref.at[0, :, at, :], weight_in.at[:, at, :], sems.at[c, 0]),
            pltpu.make_async_copy(act_ref.at[0, theirs, :, at], act.at[:, :, at], sems.at[c, 1]),
            pltpu.make_async_copy(out_ref.at[0, :, :, at], weight_out.at[:, :, at], sems.at[c, 2]),
            pltpu.make_async_copy(grad_ref.at[0, theirs, :, at], grad.at[:, :, at], sems.at[c, 3]),
        ]

    later = [
        pltpu.make_async_copy(act_ref.at[0, mine], act_mine, mine_sems.at[0]),
        pltpu.make_async_copy(grad_ref.at[0, mine], grad_mine, mine_sems.at[1]),
    ]
    for c in range(len(spans)):
        for copy in copies(c):
            copy.start()
    for copy in later:
        copy.start()
    sums = None
    for c in range(len(spans)):
        for copy in copies(c):
            copy.wait()
        parts = project(act, grad, weight_in, weight_out, *spans[c])
        sums = parts if sums is None else [s + p for s, p in zip(sums, parts)]
    write_terms(sums, theirs_ref, term)
    for copy in later:
        copy.wait()


def mine_kernel(act, grad, weight_in, weight_out, mine_ref, term):
    sums = None
    size = 1024
    for first in range(0, act.shape[2], size):
        parts = project(act, grad, weight_in, weight_out, first, size)
        sums = parts if sums is None else [s + p for s, p in zip(sums, parts)]
    write_terms(sums, mine_ref, term)


def layer_terms(activations, out_grads, proj_in, proj_out):
    count, length, width = activations.shape[1:]
    half = count // C
    k_in, k_out = proj_in.shape[3], proj_out.shape[2]
    piece = jax.ShapeDtypeStruct((k_out // PAIRS, PAIRS * half, k_in), F32)
    tokens = jax.ShapeDtypeStruct((half, length, width), jnp.bfloat16)
    vmem = pl.BlockSpec(memory_space=pltpu.VMEM)
    theirs, *kept = pl.pallas_call(
        theirs_kernel,
        in_specs=[pl.BlockSpec(memory_space=pl.ANY)] * 4,
        out_specs=[vmem] * 5,
        out_shape=[
            piece,
            tokens,
            tokens,
            jax.ShapeDtypeStruct(proj_in.shape[1:], jnp.bfloat16),
            jax.ShapeDtypeStruct(proj_out.shape[1:], jnp.bfloat16),
        ],
        scratch_shapes=[
            pltpu.VMEM(tokens.shape, jnp.bfloat16),
            pltpu.VMEM(tokens.shape, jnp.bfloat16),
            pltpu.VMEM((half, k_out, k_in), F32),
            pltpu.SemaphoreType.DMA((len(CHUNKS), 4)),
            pltpu.SemaphoreType.DMA((2,)),
        ],
        compiler_params=pltpu.CompilerParams(vmem_limit_bytes=VMEM_BYTES),
    )(*(pltpu.with_memory_space_constraint(a, pltpu.HBM) for a in (activations, out_grads, proj_in, proj_out)))
    mine = pl.pallas_call(
        mine_kernel,
        in_specs=[vmem] * 4,
        out_specs=vmem,
        out_shape=piece,
        scratch_shapes=[pltpu.VMEM((half, k_out, k_in), F32)],
        cost_estimate=pl.CostEstimate(
            flops=2 * half * length * width * PROJ * (k_in + k_out),
            bytes_accessed=8 * 2**20,
            transcendentals=0,
        ),
        compiler_params=pltpu.CompilerParams(vmem_limit_bytes=16 * 2**20),
    )(*kept)
    return mine, theirs


def thirds(value):
    parts = []
    for _ in range(3):
        part = value.astype(jnp.bfloat16)
        parts.append(part)
        value = value - part.astype(F32)
    return parts


def pack_kernel(ref_0, ref_1, ref_2, ref_3, packed_ref, reduced):
    zh = lax.div(lax.axis_index("section"), Y * C)
    reduced[...] = (ref_0[...] + ref_1[...]) + (ref_2[...] + ref_3[...])
    half = reduced.shape[0] // PAIRS
    for y in range(Y):
        row = reduced[pl.ds(pl.multiple_of((zh * Y + y) * half, half), half), :]
        for d in range(GROUPS):
            at = (Y_RANKS.index(y) * GROUPS + D_RANKS.index(d)) * SHARE * half
            packed_ref[at : at + half, :] = row
            packed_ref[at + half : at + SHARE * half, :] = reduced[
                d * 2 * half : (d + 1) * 2 * half, :
            ]


def pack(pieces):
    shape = pieces[0].shape
    return pl.pallas_call(
        pack_kernel,
        in_specs=[pl.BlockSpec(memory_space=pltpu.VMEM)] * ZH,
        out_specs=pl.BlockSpec(memory_space=pltpu.VMEM),
        out_shape=jax.ShapeDtypeStruct(
            (Y * GROUPS * SHARE * (shape[0] // PAIRS), shape[1]), F32
        ),
        scratch_shapes=[pltpu.VMEM(shape, F32)],
        compiler_params=pltpu.CompilerParams(vmem_limit_bytes=8 * 2**20),
    )(*pieces)


def y_rank(k):
    if isinstance(k, int):
        return Y_RANKS.index(k)
    return sum(at * (k == y).astype(jnp.int32) for at, y in enumerate(Y_RANKS))


def gathered(ref, k, row):
    half = ref.shape[0] // (Y * GROUPS * SHARE)
    return jnp.concatenate(
        [
            ref[pl.ds((y_rank(k) * GROUPS * SHARE + row) * half + e, GROUPS, stride=SHARE * half), :]
            for e in range(half)
        ],
        axis=0,
    )


def factors(ref, core, scale):
    r = thirds(
        jnp.concatenate([gathered(ref, core * 2 + k, 0) for k in range(2)], axis=1) * scale
    )
    c = thirds(
        jnp.concatenate([gathered(ref, k, 1 + j) for j in range(2) for k in range(4)], axis=1)
    )
    pairs = [(0, 0), (0, 1), (1, 0), (1, 1), (0, 2), (2, 0)]
    return (
        jnp.concatenate([r[i] for i, _ in pairs], axis=0),
        jnp.concatenate([c[j] for _, j in pairs], axis=0),
    )


def outer_product(ref, core, scale):
    rows, cols = factors(ref, core, scale)
    return lax.dot_general(
        rows, cols, (((0,), (0,)), ((), ())), preferred_element_type=F32
    )


def near_kernel(scale, ref, earlier_ref, held_ref):
    core = lax.rem(lax.axis_index("section"), C)
    held_ref[...] = earlier_ref[...] + outer_product(ref, core, scale)


def far_kernel(scale, ref, held_ref, gram_ref, total, sems):
    core = lax.rem(lax.axis_index("section"), C)
    rows, cols = factors(ref, core, scale)
    count = sems.shape[0]
    size = total.shape[0] // count
    copies = []
    for i in range(count):
        at = slice(i * size, (i + 1) * size)
        total[at, :] = held_ref[at, :] + lax.dot_general(
            rows[:, at], cols, (((0,), (0,)), ((), ())), preferred_element_type=F32
        )
        copy = pltpu.make_async_copy(total.at[at, :], gram_ref.at[at, :], sems.at[i])
        copy.start()
        copies.append(copy)
    for copy in copies:
        copy.wait()


def add_near(scale, features, earlier_gram):
    shape = earlier_gram.shape
    return pl.pallas_call(
        functools.partial(near_kernel, scale),
        in_specs=[pl.BlockSpec(memory_space=pltpu.VMEM)] * 2,
        out_specs=pl.BlockSpec(memory_space=pltpu.VMEM),
        out_shape=jax.ShapeDtypeStruct(shape, F32),
        cost_estimate=pl.CostEstimate(
            flops=12 * shape[0] * shape[1] * 32,
            bytes_accessed=4 * shape[0] * shape[1],
            transcendentals=0,
        ),
        compiler_params=pltpu.CompilerParams(vmem_limit_bytes=16 * 2**20),
    )(features, earlier_gram)


def add_far(scale, features, held):
    return pl.pallas_call(
        functools.partial(far_kernel, scale),
        in_specs=[pl.BlockSpec(memory_space=pltpu.VMEM)] * 2,
        out_specs=pl.BlockSpec(memory_space=pl.ANY),
        out_shape=jax.ShapeDtypeStruct(held.shape, F32),
        scratch_shapes=[
            pltpu.VMEM(held.shape, F32),
            pltpu.SemaphoreType.DMA((OUT_PARTS,)),
        ],
        compiler_params=pltpu.CompilerParams(vmem_limit_bytes=16 * 2**20),
    )(features, held)


def per_device(activations, out_grads, proj_in, proj_out, earlier_gram):
    mine, theirs = layer_terms(activations, out_grads, proj_in, proj_out)
    mine = mine + lax.ppermute(theirs, "section", ACROSS_CORES)
    reduced = mine[0]
    for turn in (2, 1, 3):
        reduced = reduced + lax.ppermute(mine[turn], "section", across(0, turn))
    pieces = [reduced] + [
        lax.ppermute(reduced, "section", across(turn, 0)) for turn in (1, 3, 2)
    ]
    packed = pack(pieces)
    rows = packed.shape[0] // (Y * GROUPS * SHARE)
    packed = packed.reshape(Y * GROUPS, SHARE, rows, LANES)
    near = lax.all_to_all(packed, BOTH, 0, 0, axis_index_groups=SAME_ZH)
    near = near.reshape(-1, LANES)
    far = lax.ppermute(near, "section", ACROSS_CORES)
    total_examples = activations.shape[1] * GROUPS
    scale = 1.0 / (LEN * SECTIONS * PROJ * total_examples)
    return add_far(scale, far, add_near(scale, near, earlier_gram))


def solution(mesh):
    return jax.shard_map(
        per_device,
        mesh=mesh,
        in_specs=(
            P("section", "dp", None, None),
            P("section", "dp", None, None),
            P("section", None, None, None),
            P("section", None, None, None),
            P("section", "dp"),
        ),
        out_specs=P("section", "dp"),
        check_vma=False,
    )
```
